32 devices in a mesh: grp: 4 (over z), fsdp: 2 (over core), tp: 4 (over y, x).
Axes of the slice: x: 2, y: 2, z: 4, core: 2. Of those that a mesh axis runs over, the one named last changes fastest.
Arguments:
- queries: bfloat16 [16, 8192], P('fsdp', 'tp'), may hold values from -96 to 96
- cache: bfloat16 [2, 16, 2048, 1024], P(None, 'fsdp', 'grp', 'tp'), may hold values from -4 to 4, as said below
- lengths: int32 [16], P('fsdp'), may hold values from 2 to 2048, as said below
- output_weight: bfloat16 [8192, 8192], P('tp'), may hold values from -0.5 to 0.5
- adapter_down_weight: bfloat16 [8192, 128], P('tp'), may hold values from -0.5 to 0.5
- adapter_up_weight: bfloat16 [128, 8192], P('fsdp', 'tp'), may hold values from -0.5 to 0.5
Outputs:
- projected: bfloat16 [16, 8192], P('fsdp', 'tp')
The draws below stay inside these ranges and needn't reach their ends.
Inputs may be any that keep to these rules, and one draw needn't show every extreme that they name: `lengths`: every row has at least two live positions, and some row has all 2048. `cache`: slot s holds the same keys and values as every slot s2 with s2 * 1 == s * 1.
All inputs are finite; a program needn't handle non-finite values.
Results may differ from the reference program's by a relative error of at most 0.015.
Values may be sent and summed in bfloat16 or wider, within the bound.
A program may use at most 128 MiB of HBM per device.

```python
import jax
import jax.numpy as jnp
from jax import lax

MODEL_WIDTH = 8192
QUERY_HEAD_COUNT = 64
KVH = 8
HEAD_SIZE = 128
ADAPTER_DIM = 128
KV_SLOTS = 8
QPS = 8
ROWS = 16
CTX = 2048


def draw_cache(key, part):
    stored = jnp.clip(jax.random.normal(jax.random.fold_in(key, 11), (2, ROWS, CTX, KVH, HEAD_SIZE), jnp.float32), -4.0, 4.0)
    copied = jnp.repeat(stored, KV_SLOTS // KVH, axis=3)
    return copied.reshape(2, ROWS, CTX, KV_SLOTS * HEAD_SIZE).astype(jnp.bfloat16)


def draw_queries(key, part):
    entries = jnp.clip(2.0 * jax.random.normal(jax.random.fold_in(key, 13), (ROWS, QUERY_HEAD_COUNT * HEAD_SIZE), jnp.float32), -8.0, 8.0)
    return entries.astype(jnp.bfloat16)


def draw_lengths(key, part):
    drawn = jax.random.randint(jax.random.fold_in(key, 15), (ROWS,), 2, CTX + 1, jnp.int32)
    longest = jax.random.randint(jax.random.fold_in(key, 16), (), 0, ROWS, jnp.int32)
    return drawn.at[longest].set(CTX)


def steps_of(rng, extent, split, smallest, top_value):
    def one(dim, blocks):
        steps = jax.random.uniform(jax.random.fold_in(jax.random.fold_in(rng, 6), dim), (blocks,), jnp.float32, smallest / len(split), top_value / len(split))
        return jnp.repeat(jnp.exp(steps), extent[dim] // blocks).reshape((-1,) + (1,) * (len(extent) - dim - 1))

    loudness = one(*split[0])
    for cut in split[1:]:
        loudness = loudness * one(*cut)
    return loudness


def normal_values(key, extent, deviation, reach, pieces=(), held_as=jnp.bfloat16):
    factor_of = steps_of(key, extent, pieces, -0.22, 0.18) if pieces else 1.0
    values = jax.random.normal(key, extent, jnp.float32) * deviation * factor_of
    return jnp.minimum(jnp.maximum(values, -reach), reach).astype(held_as)


def setup_inputs(seed: int = 0) -> dict:
    splits = jax.random.split(jax.random.key(seed), 7)
    return {
        "queries": draw_queries(jax.random.fold_in(splits[6], 71), 0),
        "cache": draw_cache(jax.random.fold_in(splits[6], 71), 0),
        "lengths": draw_lengths(jax.random.fold_in(splits[6], 71), 0),
        "output_weight": normal_values(splits[3], (QUERY_HEAD_COUNT * HEAD_SIZE, MODEL_WIDTH), HEAD_SIZE ** -0.5, 0.5, ((0, 4),)),
        "adapter_down_weight": normal_values(splits[4], (QUERY_HEAD_COUNT * HEAD_SIZE, ADAPTER_DIM), HEAD_SIZE ** -0.5, 0.5, ((0, 4),)),
        "adapter_up_weight": normal_values(splits[5], (ADAPTER_DIM, MODEL_WIDTH), HEAD_SIZE ** -0.5, 0.5, ((0, 2), (1, 4))),
    }


adapter_scale = 0.5
mask_fill = -1e30


def attend_row(inputs):
    query_row, key_row, value_row, length = inputs
    query_heads = query_row.astype(jnp.float32).reshape(KV_SLOTS, QPS, HEAD_SIZE)
    key_heads = key_row.astype(jnp.float32).reshape(CTX, KV_SLOTS, HEAD_SIZE)
    value_heads = value_row.astype(jnp.float32).reshape(CTX, KV_SLOTS, HEAD_SIZE)
    scores = jnp.einsum("sqd,psd->sqp", query_heads, key_heads) * (HEAD_SIZE ** -0.5)
    visible = jnp.arange(CTX, dtype=jnp.int32) < length
    scores = jnp.where(visible, scores, mask_fill)
    best = jnp.max(scores, axis=-1, keepdims=True)
    weights = jnp.where(visible, jnp.exp(scores - best), 0.0)
    totals = jnp.sum(weights, axis=-1, keepdims=True)
    rounded = lax.optimization_barrier(weights.astype(jnp.bfloat16)).astype(jnp.float32)
    summed = jnp.einsum("sqp,psd->sqd", rounded, value_heads)
    return (summed / totals).astype(jnp.bfloat16).reshape(QUERY_HEAD_COUNT * HEAD_SIZE)


def reference(queries, cache, lengths, output_weight, adapter_down_weight, adapter_up_weight):
    flattened_heads = lax.map(attend_row, (queries, cache[0], cache[1], lengths))
    projected = jnp.dot(flattened_heads, output_weight, preferred_element_type=jnp.float32)
    adapter_output = jnp.dot(flattened_heads, adapter_down_weight, preferred_element_type=jnp.float32)
    projected = projected + adapter_scale * jnp.dot(adapter_output, adapter_up_weight.astype(jnp.float32), precision=lax.Precision.HIGHEST)
    return projected.astype(jnp.bfloat16)
```

```python
import functools
import math

import jax
import jax.numpy as jnp
from jax import lax
from jax.experimental import pallas as pl
from jax.experimental.pallas import tpu as pltpu
from jax.sharding import PartitionSpec as P

HEAD_SIZE = 128
adapter_scale = 0.5
mask_fill = -1e30
LANES = 128
MESH = pl.DeviceIdType.MESH


def pack(value):
    c = value.shape[1]
    if c % (2 * LANES) == 0:
        both = jnp.concatenate([value[:, : c // 2], value[:, c // 2 :]], axis=0)
    else:
        both = jnp.concatenate([value, jnp.zeros_like(value)], axis=0)
    return both.astype(jnp.bfloat16)


def unpack(both, c):
    both = both.astype(jnp.float32)
    rows = both.shape[0] // 2
    if c % (2 * LANES) == 0:
        return jnp.concatenate([both[:rows], both[rows:]], axis=1)
    return both[:rows]


def kernel(
    sizes,
    lengths_ref,
    queries_hbm,
    cache_hbm,
    weight_hbm,
    down_hbm,
    up_hbm,
    out_ref,
    q_buf,
    q_heads,
    cache_buf,
    weight_buf,
    down_buf,
    up_buf,
    mine_u,
    mine_s,
    got_u,
    got_s,
    att,
    part_out,
    part_in,
    rank_out,
    rank_in,
    cols,
    q_sem,
    cache_sem,
    weight_sem,
    down_sem,
    up_sem,
    up_send,
    up_recv,
    u_send,
    u_recv,
    s_send,
    s_recv,
    part_send,
    part_recv,
    rank_send,
    rank_recv,
    cols_send,
    cols_recv,
):
    grp, fsdp, tp, rows, heads, slots, ctx, split, piece, groups, padded = sizes
    per_slot = heads // slots
    group_rows = rows // groups
    width = slots * HEAD_SIZE
    here = lax.axis_index("grp")
    side = lax.axis_index("fsdp")
    place = lax.axis_index("tp")
    part = lax.rem(here, split)

    barrier = pltpu.get_barrier_semaphore()
    for axis, size, at in (("grp", grp, here), ("fsdp", fsdp, side), ("tp", tp, place)):
        for step in range(1, size):
            pl.semaphore_signal(
                barrier, inc=1, device_id={axis: lax.rem(at + step, size)}, device_id_type=MESH
            )

    q_copy = pltpu.make_async_copy(queries_hbm, q_buf, q_sem)
    q_copy.start()
    cache_copies = []
    for n in range(groups):
        these = pl.ds(n * group_rows, group_rows)
        for kv in range(2):
            copy = pltpu.make_async_copy(
                cache_hbm.at[kv, these], cache_buf.at[kv, these], cache_sem.at[n, kv]
            )
            copy.start()
            cache_copies.append(copy)
    up_copy = pltpu.make_async_copy(
        up_hbm.at[:, pl.ds(pl.multiple_of(part * piece, LANES), piece)], up_buf.at[side], up_sem
    )
    up_copy.start()
    down_copy = pltpu.make_async_copy(down_hbm, down_buf, down_sem)
    down_copy.start()
    weight_copies = []
    for step in list(range(1, tp)) + [0]:
        target = lax.rem(place + step, tp)
        at = pl.multiple_of(target * (split * piece) + part * piece, LANES)
        copy = pltpu.make_async_copy(
            weight_hbm.at[:, pl.ds(at, piece)], weight_buf.at[step], weight_sem.at[step]
        )
        copy.start()
        weight_copies.append((step, copy))

    q_copy.wait()
    if padded != heads:
        q_heads[...] = jnp.zeros_like(q_heads)
    for h in range(heads):
        q_heads[:, h, :] = q_buf[:, h * HEAD_SIZE : (h + 1) * HEAD_SIZE].astype(jnp.float32)
    head_of = lax.broadcasted_iota(jnp.int32, (padded, HEAD_SIZE), 0)
    positions = here * ctx + lax.broadcasted_iota(jnp.int32, (padded, ctx), 1)
    lane = lax.broadcasted_iota(jnp.int32, (padded, LANES), 1)
    stats = jnp.full((padded, LANES), mask_fill, jnp.float32)
    for n in range(groups):
        cache_copies[2 * n].wait()
        each = range(n * group_rows, (n + 1) * group_rows)
        weights, totals = {}, {}
        for r in each:
            q = q_heads[r]
            blocks = [
                jnp.where((head_of >= s * per_slot) & (head_of < (s + 1) * per_slot), q, 0.0)
                for s in range(slots)
            ]
            spread = jnp.concatenate(blocks, axis=1).astype(jnp.bfloat16)
            scores = lax.dot_general(
                spread,
                cache_buf[0, r],
                (((1,), (1,)), ((), ())),
                preferred_element_type=jnp.float32,
            )
            scores = scores * HEAD_SIZE ** (-0.5)
            visible = positions < lengths_ref[r]
            scores = jnp.where(visible, scores, mask_fill)
            best = jnp.max(scores, axis=1, keepdims=True)
            weight = jnp.where(visible, jnp.exp(scores - best), 0.0)
            total = jnp.sum(weight, axis=1, keepdims=True)
            total = jnp.maximum(total, 1.0)
            stats = jnp.where(lane == r, best + jnp.log(total), stats)
            weights[r] = weight.astype(jnp.bfloat16)
            totals[r] = total
        cache_copies[2 * n + 1].wait()
        for r in each:
            summed = jnp.dot(weights[r], cache_buf[1, r], preferred_element_type=jnp.float32)
            mixed = summed[:, :HEAD_SIZE]
            for s in range(1, slots):
                mixed = jnp.where(
                    head_of >= s * per_slot, summed[:, s * HEAD_SIZE : (s + 1) * HEAD_SIZE], mixed
                )
            mine_u[r * padded : (r + 1) * padded] = (mixed / totals[r]).astype(jnp.bfloat16)
    mine_s[...] = stats

    up_copy.wait()
    pl.semaphore_wait(barrier, grp + fsdp + tp - 3)

    def send(src, dst, send_sem, recv_sem, target):
        copy = pltpu.make_async_remote_copy(
            src_ref=src,
            dst_ref=dst,
            send_sem=send_sem,
            recv_sem=recv_sem,
            device_id=target,
            device_id_type=MESH,
        )
        copy.start()
        return copy

    merges = []
    for step in range(1, grp):
        target = {"grp": lax.rem(here + step, grp)}
        k = step - 1
        merges.append(send(mine_s, got_s.at[k], s_send.at[k], s_recv.at[k], target))
        merges.append(send(mine_u, got_u.at[k], u_send.at[k], u_recv.at[k], target))
    ups = []
    for step in range(1, fsdp):
        target = {"fsdp": lax.rem(side + step, fsdp)}
        k = step - 1
        ups.append(send(up_buf.at[side], up_buf.at[side], up_send.at[k], up_recv.at[k], target))

    for k in range(grp - 1):
        merges[2 * k].wait_recv()
    shares = [mine_s[...]] + [got_s[k] for k in range(grp - 1)]
    top = functools.reduce(jnp.maximum, shares)
    shares = [jnp.exp(share - top) for share in shares]
    whole = functools.reduce(jnp.add, shares)
    shares = [share / whole for share in shares]
    for k in range(grp - 1):
        merges[2 * k + 1].wait_recv()
    for r in range(rows):
        these = slice(r * padded, (r + 1) * padded)
        value = mine_u[these].astype(jnp.float32) * shares[0][:, r : r + 1]
        for k in range(grp - 1):
            value = value + got_u[k, these].astype(jnp.float32) * shares[k + 1][:, r : r + 1]
        att[r] = value
    x = jnp.concatenate([att[:, h, :] for h in range(heads)], axis=1).astype(jnp.bfloat16)

    down_copy.wait()
    rank = jnp.dot(x, down_buf[...], preferred_element_type=jnp.float32)
    rank_out[...] = rank
    ranks = []
    for step in range(1, tp):
        target = {"tp": lax.rem(place + step, tp)}
        k = step - 1
        ranks.append(send(rank_out, rank_in.at[k], rank_send.at[k], rank_recv.at[k], target))
    parts = []
    own = None
    for step, copy in weight_copies:
        copy.wait()
        product = jnp.dot(x, weight_buf[step], preferred_element_type=jnp.float32)
        if step == 0:
            own = product
        else:
            k = step - 1
            target = {"tp": lax.rem(place + step, tp)}
            part_out[k] = pack(product)
            parts.append(
                send(part_out.at[k], part_in.at[k], part_send.at[k], part_recv.at[k], target)
            )

    for copy in ups:
        copy.wait_recv()
    for k in range(tp - 1):
        ranks[k].wait_recv()
        rank = rank + rank_in[k]
    high = rank.astype(jnp.bfloat16).astype(jnp.float32)
    middle = (rank - high).astype(jnp.bfloat16).astype(jnp.float32)
    low = rank - high - middle
    pieces = jnp.concatenate([high, middle, low], axis=0).astype(jnp.bfloat16)
    second = jnp.concatenate([up_buf[i] for i in range(fsdp)], axis=0)
    adapted = jnp.dot(pieces, second, preferred_element_type=jnp.float32)
    adapted = adapted[:rows] + adapted[rows : 2 * rows] + adapted[2 * rows :]
    result = own + adapter_scale * adapted
    for k in range(tp - 1):
        parts[k].wait_recv()
        result = result + unpack(part_in[k], piece)
    cols[part] = pack(result)

    gathers = []
    for step in range(1, split):
        target = {"grp": here - part + lax.rem(part + step, split)}
        k = step - 1
        gathers.append(
            send(cols.at[part], cols.at[part], cols_send.at[k], cols_recv.at[k], target)
        )
    for copy in merges + ups + ranks + parts:
        copy.wait_send()
    for step in range(1, split):
        source = lax.rem(part - step + split, split)
        k = step - 1
        pltpu.make_async_remote_copy(
            src_ref=cols.at[source],
            dst_ref=cols.at[source],
            send_sem=cols_send.at[k],
            recv_sem=cols_recv.at[k],
            device_id={"grp": here - part + source},
            device_id_type=MESH,
        ).wait_recv()
    for n in range(split):
        out_ref[:, n * piece : (n + 1) * piece] = unpack(cols[n], piece).astype(out_ref.dtype)
    for copy in gathers:
        copy.wait_send()


def per_device(sizes, queries, cache, lengths, weight, down, up):
    grp, fsdp, tp, rows, heads, slots, ctx, split, piece, groups, padded = sizes
    bf16, f32 = jnp.bfloat16, jnp.float32
    packed = (2 * rows, piece // 2 if piece % (2 * LANES) == 0 else piece)
    rank = down.shape[1]
    dma = pltpu.SemaphoreType.DMA
    some = lambda n: max(n, 1)
    return pl.pallas_call(
        functools.partial(kernel, sizes),
        out_shape=jax.ShapeDtypeStruct((rows, split * piece), bf16),
        in_specs=[pl.BlockSpec(memory_space=pltpu.SMEM)]
        + [pl.BlockSpec(memory_space=pltpu.HBM)] * 5,
        out_specs=pl.BlockSpec(memory_space=pltpu.VMEM),
        scratch_shapes=[
            pltpu.VMEM(queries.shape, bf16),
            pltpu.VMEM((rows, padded, HEAD_SIZE), f32),
            pltpu.VMEM(cache.shape, bf16),
            pltpu.VMEM((tp, weight.shape[0], piece), bf16),
            pltpu.VMEM(down.shape, bf16),
            pltpu.VMEM((fsdp, up.shape[0], piece), bf16),
            pltpu.VMEM((rows * padded, HEAD_SIZE), bf16),
            pltpu.VMEM((padded, LANES), f32),
            pltpu.VMEM((some(grp - 1), rows * padded, HEAD_SIZE), bf16),
            pltpu.VMEM((some(grp - 1), padded, LANES), f32),
            pltpu.VMEM((rows, padded, HEAD_SIZE), f32),
            pltpu.VMEM((some(tp - 1),) + packed, bf16),
            pltpu.VMEM((some(tp - 1),) + packed, bf16),
            pltpu.VMEM((rows, rank), f32),
            pltpu.VMEM((some(tp - 1), rows, rank), f32),
            pltpu.VMEM((split,) + packed, bf16),
            dma,
            dma((groups, 2)),
            dma((tp,)),
            dma,
            dma,
            dma((some(fsdp - 1),)),
            dma((some(fsdp - 1),)),
        ]
        + [dma((some(grp - 1),))] * 4
        + [dma((some(tp - 1),))] * 4
        + [dma((some(split - 1),))] * 2,
        compiler_params=pltpu.CompilerParams(
            collective_id=0, has_side_effects=True, vmem_limit_bytes=63 * 2**20
        ),
        name="decode_step",
    )(lengths, queries, cache, weight, down, up)


def solution(mesh):
    grp, fsdp, tp = (mesh.shape[axis] for axis in ("grp", "fsdp", "tp"))
    placed = (
        P("fsdp", "tp"),
        P(None, "fsdp", "grp", "tp"),
        P("fsdp"),
        P("tp", None),
        P("tp", None),
        P("fsdp", "tp"),
    )

    def local(queries, cache, lengths, weight, down, up):
        rows, width = queries.shape
        heads = width // HEAD_SIZE
        slots = cache.shape[3] // HEAD_SIZE
        columns = up.shape[1]
        split = math.gcd(grp, columns // LANES)
        groups = math.gcd(rows, 2)
        padded = -(-heads // 16) * 16
        sizes = (
            grp, fsdp, tp, rows, heads, slots, cache.shape[2], split, columns // split, groups, padded
        )
        return per_device(sizes, queries, cache, lengths, weight, down, up)

    return jax.shard_map(
        local, mesh=mesh, in_specs=placed, out_specs=P("fsdp", "tp"), check_vma=False
    )
```

```python
import functools
import math

import jax
import jax.numpy as jnp
from jax import lax
from jax.experimental import pallas as pl
from jax.experimental.pallas import tpu as pltpu
from jax.sharding import PartitionSpec as P

HEAD_SIZE = 128
adapter_scale = 0.5
mask_fill = -1e30
LANES = 128
MESH = pl.DeviceIdType.MESH


def pack(value):
    c = value.shape[1]
    if c % (2 * LANES) == 0:
        both = jnp.concatenate([value[:, : c // 2], value[:, c // 2 :]], axis=0)
    else:
        both = jnp.concatenate([value, jnp.zeros_like(value)], axis=0)
    return both.astype(jnp.bfloat16)


def unpack(both, c):
    both = both.astype(jnp.float32)
    rows = both.shape[0] // 2
    if c % (2 * LANES) == 0:
        return jnp.concatenate([both[:rows], both[rows:]], axis=1)
    return both[:rows]


def kernel(
    sizes,
    lengths_ref,
    queries_hbm,
    cache_hbm,
    weight_hbm,
    down_hbm,
    up_hbm,
    out_ref,
    q_buf,
    q_heads,
    cache_buf,
    weight_buf,
    down_buf,
    up_buf,
    mine_u,
    mine_s,
    got_u,
    got_s,
    att,
    part_out,
    part_in,
    rank_out,
    rank_in,
    cols,
    q_sem,
    cache_sem,
    weight_sem,
    down_sem,
    up_sem,
    up_send,
    up_recv,
    u_send,
    u_recv,
    s_send,
    s_recv,
    part_send,
    part_recv,
    rank_send,
    rank_recv,
    cols_send,
    cols_recv,
):
    grp, fsdp, tp, rows, heads, slots, ctx, split, piece, groups, padded = sizes
    per_slot = heads // slots
    group_rows = rows // groups
    width = slots * HEAD_SIZE
    here = lax.axis_index("grp")
    side = lax.axis_index("fsdp")
    place = lax.axis_index("tp")
    part = lax.rem(here, split)

    barrier = pltpu.get_barrier_semaphore()
    for axis, size, at in (("grp", grp, here), ("fsdp", fsdp, side), ("tp", tp, place)):
        for step in range(1, size):
            pl.semaphore_signal(
                barrier, inc=1, device_id={axis: lax.rem(at + step, size)}, device_id_type=MESH
            )

    q_copy = pltpu.make_async_copy(queries_hbm, q_buf, q_sem)
    q_copy.start()
    cache_copies = []
    for n in range(groups):
        these = pl.ds(n * group_rows, group_rows)
        for kv in range(2):
            copy = pltpu.make_async_copy(
                cache_hbm.at[kv, these], cache_buf.at[kv, these], cache_sem.at[n, kv]
            )
            copy.start()
            cache_copies.append(copy)
    up_copy = pltpu.make_async_copy(
        up_hbm.at[:, pl.ds(pl.multiple_of(part * piece, LANES), piece)], up_buf.at[side], up_sem
    )
    up_copy.start()
    down_copy = pltpu.make_async_copy(down_hbm, down_buf, down_sem)
    down_copy.start()
    q_copy.wait()
    if padded != heads:
        q_heads[...] = jnp.zeros_like(q_heads)
    for h in range(heads):
        q_heads[:, h, :] = q_buf[:, h * HEAD_SIZE : (h + 1) * HEAD_SIZE].astype(jnp.float32)
    head_of = lax.broadcasted_iota(jnp.int32, (padded, HEAD_SIZE), 0)
    positions = here * ctx + lax.broadcasted_iota(jnp.int32, (padded, ctx), 1)
    lane = lax.broadcasted_iota(jnp.int32, (padded, LANES), 1)
    stats = jnp.full((padded, LANES), mask_fill, jnp.float32)
    for n in range(groups):
        cache_copies[2 * n].wait()
        each = range(n * group_rows, (n + 1) * group_rows)
        weights, totals = {}, {}
        for r in each:
            q = q_heads[r]
            blocks = [
                jnp.where((head_of >= s * per_slot) & (head_of < (s + 1) * per_slot), q, 0.0)
                for s in range(slots)
            ]
            spread = jnp.concatenate(blocks, axis=1).astype(jnp.bfloat16)
            scores = lax.dot_general(
                spread,
                cache_buf[0, r],
                (((1,), (1,)), ((), ())),
                preferred_element_type=jnp.float32,
            )
            scores = scores * HEAD_SIZE ** (-0.5)
            visible = positions < lengths_ref[r]
            scores = jnp.where(visible, scores, mask_fill)
            best = jnp.max(scores, axis=1, keepdims=True)
            weight = jnp.where(visible, jnp.exp(scores - best), 0.0)
            total = jnp.sum(weight, axis=1, keepdims=True)
            total = jnp.maximum(total, 1.0)
            stats = jnp.where(lane == r, best + jnp.log(total), stats)
            weights[r] = weight.astype(jnp.bfloat16)
            totals[r] = total
        cache_copies[2 * n + 1].wait()
        if n == groups - 1:
            weight_copies = []
            for step in list(range(1, tp)) + [0]:
                target = lax.rem(place + step, tp)
                at = pl.multiple_of(target * (split * piece) + part * piece, LANES)
                copy = pltpu.make_async_copy(
                    weight_hbm.at[:, pl.ds(at, piece)], weight_buf.at[step], weight_sem.at[step]
                )
                copy.start()
                weight_copies.append((step, copy))
        for r in each:
            summed = jnp.dot(weights[r], cache_buf[1, r], preferred_element_type=jnp.float32)
            mixed = summed[:, :HEAD_SIZE]
            for s in range(1, slots):
                mixed = jnp.where(
                    head_of >= s * per_slot, summed[:, s * HEAD_SIZE : (s + 1) * HEAD_SIZE], mixed
                )
            mine_u[r * padded : (r + 1) * padded] = (mixed / totals[r]).astype(jnp.bfloat16)
    mine_s[...] = stats

    up_copy.wait()
    pl.semaphore_wait(barrier, grp + fsdp + tp - 3)

    def send(src, dst, send_sem, recv_sem, target):
        copy = pltpu.make_async_remote_copy(
            src_ref=src,
            dst_ref=dst,
            send_sem=send_sem,
            recv_sem=recv_sem,
            device_id=target,
            device_id_type=MESH,
        )
        copy.start()
        return copy

    merges = []
    for step in range(1, grp):
        target = {"grp": lax.rem(here + step, grp)}
        k = step - 1
        merges.append(send(mine_s, got_s.at[k], s_send.at[k], s_recv.at[k], target))
        merges.append(send(mine_u, got_u.at[k], u_send.at[k], u_recv.at[k], target))
    ups = []
    for step in range(1, fsdp):
        target = {"fsdp": lax.rem(side + step, fsdp)}
        k = step - 1
        ups.append(send(up_buf.at[side], up_buf.at[side], up_send.at[k], up_recv.at[k], target))

    for k in range(grp - 1):
        merges[2 * k].wait_recv()
    shares = [mine_s[...]] + [got_s[k] for k in range(grp - 1)]
    top = functools.reduce(jnp.maximum, shares)
    shares = [jnp.exp(share - top) for share in shares]
    whole = functools.reduce(jnp.add, shares)
    shares = [share / whole for share in shares]
    for k in range(grp - 1):
        merges[2 * k + 1].wait_recv()
    for r in range(rows):
        these = slice(r * padded, (r + 1) * padded)
        value = mine_u[these].astype(jnp.float32) * shares[0][:, r : r + 1]
        for k in range(grp - 1):
            value = value + got_u[k, these].astype(jnp.float32) * shares[k + 1][:, r : r + 1]
        att[r] = value
    x = jnp.concatenate([att[:, h, :] for h in range(heads)], axis=1).astype(jnp.bfloat16)

    down_copy.wait()
    rank = jnp.dot(x, down_buf[...], preferred_element_type=jnp.float32)
    rank_out[...] = rank
    ranks = []
    for step in range(1, tp):
        target = {"tp": lax.rem(place + step, tp)}
        k = step - 1
        ranks.append(send(rank_out, rank_in.at[k], rank_send.at[k], rank_recv.at[k], target))
    parts = []
    own = None
    for step, copy in weight_copies:
        copy.wait()
        product = jnp.dot(x, weight_buf[step], preferred_element_type=jnp.float32)
        if step == 0:
            own = product
        else:
            k = step - 1
            target = {"tp": lax.rem(place + step, tp)}
            part_out[k] = pack(product)
            parts.append(
                send(part_out.at[k], part_in.at[k], part_send.at[k], part_recv.at[k], target)
            )

    for copy in ups:
        copy.wait_recv()
    for k in range(tp - 1):
        ranks[k].wait_recv()
        rank = rank + rank_in[k]
    high = rank.astype(jnp.bfloat16).astype(jnp.float32)
    middle = (rank - high).astype(jnp.bfloat16).astype(jnp.float32)
    low = rank - high - middle
    pieces = jnp.concatenate([high, middle, low], axis=0).astype(jnp.bfloat16)
    second = jnp.concatenate([up_buf[i] for i in range(fsdp)], axis=0)
    adapted = jnp.dot(pieces, second, preferred_element_type=jnp.float32)
    adapted = adapted[:rows] + adapted[rows : 2 * rows] + adapted[2 * rows :]
    result = own + adapter_scale * adapted
    for k in range(tp - 1):
        parts[k].wait_recv()
        result = result + unpack(part_in[k], piece)
    cols[part] = pack(result)

    gathers = []
    for step in range(1, split):
        target = {"grp": here - part + lax.rem(part + step, split)}
        k = step - 1
        gathers.append(
            send(cols.at[part], cols.at[part], cols_send.at[k], cols_recv.at[k], target)
        )
    for copy in merges + ups + ranks + parts:
        copy.wait_send()
    for step in range(1, split):
        source = lax.rem(part - step + split, split)
        k = step - 1
        pltpu.make_async_remote_copy(
            src_ref=cols.at[source],
            dst_ref=cols.at[source],
            send_sem=cols_send.at[k],
            recv_sem=cols_recv.at[k],
            device_id={"grp": here - part + source},
            device_id_type=MESH,
        ).wait_recv()
    for n in range(split):
        out_ref[:, n * piece : (n + 1) * piece] = unpack(cols[n], piece).astype(out_ref.dtype)
    for copy in gathers:
        copy.wait_send()


def per_device(sizes, queries, cache, lengths, weight, down, up):
    grp, fsdp, tp, rows, heads, slots, ctx, split, piece, groups, padded = sizes
    bf16, f32 = jnp.bfloat16, jnp.float32
    packed = (2 * rows, piece // 2 if piece % (2 * LANES) == 0 else piece)
    rank = down.shape[1]
    dma = pltpu.SemaphoreType.DMA
    some = lambda n: max(n, 1)
    return pl.pallas_call(
        functools.partial(kernel, sizes),
        out_shape=jax.ShapeDtypeStruct((rows, split * piece), bf16),
        in_specs=[pl.BlockSpec(memory_space=pltpu.SMEM)]
        + [pl.BlockSpec(memory_space=pltpu.HBM)] * 5,
        out_specs=pl.BlockSpec(memory_space=pltpu.VMEM),
        scratch_shapes=[
            pltpu.VMEM(queries.shape, bf16),
            pltpu.VMEM((rows, padded, HEAD_SIZE), f32),
            pltpu.VMEM(cache.shape, bf16),
            pltpu.VMEM((tp, weight.shape[0], piece), bf16),
            pltpu.VMEM(down.shape, bf16),
            pltpu.VMEM((fsdp, up.shape[0], piece), bf16),
            pltpu.VMEM((rows * padded, HEAD_SIZE), bf16),
            pltpu.VMEM((padded, LANES), f32),
            pltpu.VMEM((some(grp - 1), rows * padded, HEAD_SIZE), bf16),
            pltpu.VMEM((some(grp - 1), padded, LANES), f32),
            pltpu.VMEM((rows, padded, HEAD_SIZE), f32),
            pltpu.VMEM((some(tp - 1),) + packed, bf16),
            pltpu.VMEM((some(tp - 1),) + packed, bf16),
            pltpu.VMEM((rows, rank), f32),
            pltpu.VMEM((some(tp - 1), rows, rank), f32),
            pltpu.VMEM((split,) + packed, bf16),
            dma,
            dma((groups, 2)),
            dma((tp,)),
            dma,
            dma,
            dma((some(fsdp - 1),)),
            dma((some(fsdp - 1),)),
        ]
        + [dma((some(grp - 1),))] * 4
        + [dma((some(tp - 1),))] * 4
        + [dma((some(split - 1),))] * 2,
        compiler_params=pltpu.CompilerParams(
            collective_id=0, has_side_effects=True, vmem_limit_bytes=63 * 2**20
        ),
        name="decode_step",
    )(lengths, queries, cache, weight, down, up)


def solution(mesh):
    grp, fsdp, tp = (mesh.shape[axis] for axis in ("grp", "fsdp", "tp"))
    placed = (
        P("fsdp", "tp"),
        P(None, "fsdp", "grp", "tp"),
        P("fsdp"),
        P("tp", None),
        P("tp", None),
        P("fsdp", "tp"),
    )

    def local(queries, cache, lengths, weight, down, up):
        rows, width = queries.shape
        heads = width // HEAD_SIZE
        slots = cache.shape[3] // HEAD_SIZE
        columns = up.shape[1]
        split = math.gcd(grp, columns // LANES)
        groups = 1
        padded = -(-heads // 16) * 16
        sizes = (
            grp, fsdp, tp, rows, heads, slots, cache.shape[2], split, columns // split, groups, padded
        )
        return per_device(sizes, queries, cache, lengths, weight, down, up)

    return jax.shard_map(
        local, mesh=mesh, in_specs=placed, out_specs=P("fsdp", "tp"), check_vma=False
    )
```

```python
import functools
import math

import jax
import jax.numpy as jnp
from jax import lax
from jax.experimental import pallas as pl
from jax.experimental.pallas import tpu as pltpu
from jax.sharding import PartitionSpec as P

HEAD_SIZE = 128
adapter_scale = 0.5
mask_fill = -1e30
LANES = 128
MESH = pl.DeviceIdType.MESH


def pack(value):
    c = value.shape[1]
    if c % (2 * LANES) == 0:
        both = jnp.concatenate([value[:, : c // 2], value[:, c // 2 :]], axis=0)
    else:
        both = jnp.concatenate([value, jnp.zeros_like(value)], axis=0)
    return both.astype(jnp.bfloat16)


def unpack(both, c):
    both = both.astype(jnp.float32)
    rows = both.shape[0] // 2
    if c % (2 * LANES) == 0:
        return jnp.concatenate([both[:rows], both[rows:]], axis=1)
    return both[:rows]


def kernel(
    sizes,
    lengths_hbm,
    queries_hbm,
    cache_hbm,
    weight_hbm,
    down_hbm,
    up_hbm,
    out_ref,
    lengths_ref,
    lengths_sem,
    q_buf,
    q_heads,
    cache_buf,
    weight_buf,
    down_buf,
    up_buf,
    mine_u,
    mine_s,
    got_u,
    got_s,
    att,
    part_out,
    part_in,
    rank_out,
    rank_in,
    cols,
    q_sem,
    cache_sem,
    weight_sem,
    down_sem,
    up_sem,
    up_send,
    up_recv,
    u_send,
    u_recv,
    s_send,
    s_recv,
    part_send,
    part_recv,
    rank_send,
    rank_recv,
    cols_send,
    cols_recv,
):
    grp, fsdp, tp, rows, heads, slots, ctx, split, piece, groups, padded = sizes
    per_slot = heads // slots
    group_rows = rows // groups
    width = slots * HEAD_SIZE
    here = lax.axis_index("grp")
    side = lax.axis_index("fsdp")
    place = lax.axis_index("tp")
    part = lax.rem(here, split)

    q_copy = pltpu.make_async_copy(queries_hbm, q_buf, q_sem)
    q_copy.start()
    lengths_copy = pltpu.make_async_copy(lengths_hbm, lengths_ref, lengths_sem)
    lengths_copy.start()
    cache_copies = []
    for n in range(groups):
        these = pl.ds(n * group_rows, group_rows)
        for kv in range(2):
            copy = pltpu.make_async_copy(
                cache_hbm.at[kv, these], cache_buf.at[kv, these], cache_sem.at[n, kv]
            )
            copy.start()
            cache_copies.append(copy)
    barrier = pltpu.get_barrier_semaphore()
    for axis, size, at in (("grp", grp, here), ("fsdp", fsdp, side), ("tp", tp, place)):
        for step in range(1, size):
            pl.semaphore_signal(
                barrier, inc=1, device_id={axis: lax.rem(at + step, size)}, device_id_type=MESH
            )

    up_copy = pltpu.make_async_copy(
        up_hbm.at[:, pl.ds(pl.multiple_of(part * piece, LANES), piece)], up_buf.at[side], up_sem
    )
    up_copy.start()
    down_copy = pltpu.make_async_copy(down_hbm, down_buf, down_sem)
    down_copy.start()
    lengths_copy.wait()
    q_copy.wait()
    if padded != heads:
        q_heads[...] = jnp.zeros_like(q_heads)
    for h in range(heads):
        q_heads[:, h, :] = q_buf[:, h * HEAD_SIZE : (h + 1) * HEAD_SIZE].astype(jnp.float32)
    head_of = lax.broadcasted_iota(jnp.int32, (padded, HEAD_SIZE), 0)
    positions = here * ctx + lax.broadcasted_iota(jnp.int32, (padded, ctx), 1)
    lane = lax.broadcasted_iota(jnp.int32, (padded, LANES), 1)
    stats = jnp.full((padded, LANES), mask_fill, jnp.float32)
    for n in range(groups):
        cache_copies[2 * n].wait()
        each = range(n * group_rows, (n + 1) * group_rows)
        weights, totals = {}, {}
        for r in each:
            q = q_heads[r]
            blocks = [
                jnp.where((head_of >= s * per_slot) & (head_of < (s + 1) * per_slot), q, 0.0)
                for s in range(slots)
            ]
            spread = jnp.concatenate(blocks, axis=1).astype(jnp.bfloat16)
            scores = lax.dot_general(
                spread,
                cache_buf[0, r],
                (((1,), (1,)), ((), ())),
                preferred_element_type=jnp.float32,
            )
            scores = scores * HEAD_SIZE ** (-0.5)
            visible = positions < lengths_ref[r]
            scores = jnp.where(visible, scores, mask_fill)
            best = jnp.max(scores, axis=1, keepdims=True)
            weight = jnp.where(visible, jnp.exp(scores - best), 0.0)
            total = jnp.sum(weight, axis=1, keepdims=True)
            total = jnp.maximum(total, 1.0)
            stats = jnp.where(lane == r, best + jnp.log(total), stats)
            weights[r] = weight.astype(jnp.bfloat16)
            totals[r] = total
        cache_copies[2 * n + 1].wait()
        if n == groups - 1:
            weight_copies = []
            for step in list(range(1, tp)) + [0]:
                target = lax.rem(place + step, tp)
                at = pl.multiple_of(target * (split * piece) + part * piece, LANES)
                copy = pltpu.make_async_copy(
                    weight_hbm.at[:, pl.ds(at, piece)], weight_buf.at[step], weight_sem.at[step]
                )
                copy.start()
                weight_copies.append((step, copy))
        for r in each:
            summed = jnp.dot(weights[r], cache_buf[1, r], preferred_element_type=jnp.float32)
            mixed = summed[:, :HEAD_SIZE]
            for s in range(1, slots):
                mixed = jnp.where(
                    head_of >= s * per_slot, summed[:, s * HEAD_SIZE : (s + 1) * HEAD_SIZE], mixed
                )
            mine_u[r * padded : (r + 1) * padded] = (mixed / totals[r]).astype(jnp.bfloat16)
    mine_s[...] = stats

    up_copy.wait()
    pl.semaphore_wait(barrier, grp + fsdp + tp - 3)

    def send(src, dst, send_sem, recv_sem, target):
        copy = pltpu.make_async_remote_copy(
            src_ref=src,
            dst_ref=dst,
            send_sem=send_sem,
            recv_sem=recv_sem,
            device_id=target,
            device_id_type=MESH,
        )
        copy.start()
        return copy

    merges = []
    for step in range(1, grp):
        target = {"grp": lax.rem(here + step, grp)}
        k = step - 1
        merges.append(send(mine_s, got_s.at[k], s_send.at[k], s_recv.at[k], target))
        merges.append(send(mine_u, got_u.at[k], u_send.at[k], u_recv.at[k], target))
    ups = []
    for step in range(1, fsdp):
        target = {"fsdp": lax.rem(side + step, fsdp)}
        k = step - 1
        ups.append(send(up_buf.at[side], up_buf.at[side], up_send.at[k], up_recv.at[k], target))

    for k in range(grp - 1):
        merges[2 * k].wait_recv()
    shares = [mine_s[...]] + [got_s[k] for k in range(grp - 1)]
    top = functools.reduce(jnp.maximum, shares)
    shares = [jnp.exp(share - top) for share in shares]
    whole = functools.reduce(jnp.add, shares)
    shares = [share / whole for share in shares]
    for k in range(grp - 1):
        merges[2 * k + 1].wait_recv()
    for r in range(rows):
        these = slice(r * padded, (r + 1) * padded)
        value = mine_u[these].astype(jnp.float32) * shares[0][:, r : r + 1]
        for k in range(grp - 1):
            value = value + got_u[k, these].astype(jnp.float32) * shares[k + 1][:, r : r + 1]
        att[r] = value
    x = jnp.concatenate([att[:, h, :] for h in range(heads)], axis=1).astype(jnp.bfloat16)

    down_copy.wait()
    rank = jnp.dot(x, down_buf[...], preferred_element_type=jnp.float32)
    rank_out[...] = rank
    ranks = []
    for step in range(1, tp):
        target = {"tp": lax.rem(place + step, tp)}
        k = step - 1
        ranks.append(send(rank_out, rank_in.at[k], rank_send.at[k], rank_recv.at[k], target))
    parts = []
    own = None
    for step, copy in weight_copies:
        copy.wait()
        product = jnp.dot(x, weight_buf[step], preferred_element_type=jnp.float32)
        if step == 0:
            own = product
        else:
            k = step - 1
            target = {"tp": lax.rem(place + step, tp)}
            part_out[k] = pack(product)
            parts.append(
                send(part_out.at[k], part_in.at[k], part_send.at[k], part_recv.at[k], target)
            )

    for copy in ups:
        copy.wait_recv()
    for k in range(tp - 1):
        ranks[k].wait_recv()
        rank = rank + rank_in[k]
    high = rank.astype(jnp.bfloat16).astype(jnp.float32)
    middle = (rank - high).astype(jnp.bfloat16).astype(jnp.float32)
    low = rank - high - middle
    pieces = jnp.concatenate([high, middle, low], axis=0).astype(jnp.bfloat16)
    second = jnp.concatenate([up_buf[i] for i in range(fsdp)], axis=0)
    adapted = jnp.dot(pieces, second, preferred_element_type=jnp.float32)
    adapted = adapted[:rows] + adapted[rows : 2 * rows] + adapted[2 * rows :]
    result = own + adapter_scale * adapted
    for k in range(tp - 1):
        parts[k].wait_recv()
        result = result + unpack(part_in[k], piece)
    cols[part] = pack(result)

    gathers = []
    for step in range(1, split):
        target = {"grp": here - part + lax.rem(part + step, split)}
        k = step - 1
        gathers.append(
            send(cols.at[part], cols.at[part], cols_send.at[k], cols_recv.at[k], target)
        )
    for copy in merges + ups + ranks + parts:
        copy.wait_send()
    for step in range(1, split):
        source = lax.rem(part - step + split, split)
        k = step - 1
        pltpu.make_async_remote_copy(
            src_ref=cols.at[source],
            dst_ref=cols.at[source],
            send_sem=cols_send.at[k],
            recv_sem=cols_recv.at[k],
            device_id={"grp": here - part + source},
            device_id_type=MESH,
        ).wait_recv()
    for n in range(split):
        out_ref[:, n * piece : (n + 1) * piece] = unpack(cols[n], piece).astype(out_ref.dtype)
    for copy in gathers:
        copy.wait_send()


def per_device(sizes, queries, cache, lengths, weight, down, up):
    grp, fsdp, tp, rows, heads, slots, ctx, split, piece, groups, padded = sizes
    bf16, f32 = jnp.bfloat16, jnp.float32
    packed = (2 * rows, piece // 2 if piece % (2 * LANES) == 0 else piece)
    rank = down.shape[1]
    dma = pltpu.SemaphoreType.DMA
    some = lambda n: max(n, 1)
    return pl.pallas_call(
        functools.partial(kernel, sizes),
        out_shape=jax.ShapeDtypeStruct((rows, split * piece), bf16),
        in_specs=[pl.BlockSpec(memory_space=pltpu.HBM)] * 6,
        out_specs=pl.BlockSpec(memory_space=pltpu.VMEM),
        scratch_shapes=[
            pltpu.SMEM(lengths.shape, jnp.int32),
            dma,
            pltpu.VMEM(queries.shape, bf16),
            pltpu.VMEM((rows, padded, HEAD_SIZE), f32),
            pltpu.VMEM(cache.shape, bf16),
            pltpu.VMEM((tp, weight.shape[0], piece), bf16),
            pltpu.VMEM(down.shape, bf16),
            pltpu.VMEM((fsdp, up.shape[0], piece), bf16),
            pltpu.VMEM((rows * padded, HEAD_SIZE), bf16),
            pltpu.VMEM((padded, LANES), f32),
            pltpu.VMEM((some(grp - 1), rows * padded, HEAD_SIZE), bf16),
            pltpu.VMEM((some(grp - 1), padded, LANES), f32),
            pltpu.VMEM((rows, padded, HEAD_SIZE), f32),
            pltpu.VMEM((some(tp - 1),) + packed, bf16),
            pltpu.VMEM((some(tp - 1),) + packed, bf16),
            pltpu.VMEM((rows, rank), f32),
            pltpu.VMEM((some(tp - 1), rows, rank), f32),
            pltpu.VMEM((split,) + packed, bf16),
            dma,
            dma((groups, 2)),
            dma((tp,)),
            dma,
            dma,
            dma((some(fsdp - 1),)),
            dma((some(fsdp - 1),)),
        ]
        + [dma((some(grp - 1),))] * 4
        + [dma((some(tp - 1),))] * 4
        + [dma((some(split - 1),))] * 2,
        compiler_params=pltpu.CompilerParams(
            collective_id=0, has_side_effects=True, vmem_limit_bytes=63 * 2**20
        ),
        name="decode_step",
    )(lengths, queries, cache, weight, down, up)


def solution(mesh):
    grp, fsdp, tp = (mesh.shape[axis] for axis in ("grp", "fsdp", "tp"))
    placed = (
        P("fsdp", "tp"),
        P(None, "fsdp", "grp", "tp"),
        P("fsdp"),
        P("tp", None),
        P("tp", None),
        P("fsdp", "tp"),
    )

    def local(queries, cache, lengths, weight, down, up):
        rows, width = queries.shape
        heads = width // HEAD_SIZE
        slots = cache.shape[3] // HEAD_SIZE
        columns = up.shape[1]
        split = 1
        groups = 1
        padded = -(-heads // 16) * 16
        sizes = (
            grp, fsdp, tp, rows, heads, slots, cache.shape[2], split, columns // split, groups, padded
        )
        return per_device(sizes, queries, cache, lengths, weight, down, up)

    return jax.shard_map(
        local, mesh=mesh, in_specs=placed, out_specs=P("fsdp", "tp"), check_vma=False
    )
```
